32 devices in a mesh: row: 4 (over y, x), col: 8 (over z, core).
Axes of the slice: x: 2, y: 2, z: 4, core: 2. Of those that a mesh axis runs over, the one named last changes fastest.
Arguments:
- pair_map: bfloat16 [640, 640, 128], P('row', 'col'), may hold values from -9 to 9
- input_gain: float32 [128], replicated, may hold values from 0.25 to 1.75
- input_bias: float32 [128], replicated, may hold values from -2.5 to 2.5
- left_weight: bfloat16 [128, 256], replicated, may hold values from -0.5 to 0.5
- left_bias: float32 [256], replicated, may hold values from -2.5 to 2.5
- right_weight: bfloat16 [128, 256], replicated, may hold values from -0.5 to 0.5
- right_bias: float32 [256], replicated, may hold values from -2.5 to 2.5
- gate_weight: bfloat16 [128, 128], replicated, may hold values from -0.5 to 0.5
- gate_bias: float32 [128], replicated, may hold values from -2.5 to 2.5
- output_gain: float32 [128], replicated, may hold values from 0.25 to 1.75
- output_bias: float32 [128], replicated, may hold values from -2.5 to 2.5
- final_weight: bfloat16 [128, 128], replicated, may hold values from -0.5 to 0.5
- final_bias: float32 [128], replicated, may hold values from -2.5 to 2.5
Outputs:
- slab_update: bfloat16 [8, 640, 128], P('row', 'col')
The draws below stay inside these ranges and needn't reach their ends.
All inputs are finite; a program needn't handle non-finite values.
Results may differ from the reference program's by a relative error of at most 0.014.
Values may be sent and summed in bfloat16 or wider, within the bound.
A program may use at most 128 MiB of HBM per device.

```python
import jax
import jax.numpy as jnp
from jax import lax

C = 128
H = 128
N = 640
SLAB = 8
N_ROW = 4


def draw_pair_map(key, part):
    key = jax.random.fold_in(key, 11)
    scale_key, entry_key = jax.random.split(key, 2)
    scales = jnp.exp(jax.random.uniform(scale_key, (C,), jnp.float32, jnp.log(0.3), jnp.log(3.0)))
    values = jnp.clip(jax.random.normal(entry_key, (N, N, C), jnp.float32), -3.0, 3.0) * scales
    return values.astype(jnp.bfloat16)


def noise(stream_key, extent, width, most, dtype=jnp.bfloat16):
    values = width * jax.random.normal(stream_key, extent, jnp.float32)
    return jnp.clip(values, min=-most, max=most).astype(dtype)


def setup_inputs(seed: int = 0) -> dict:
    streams_of = jax.random.split(jax.random.key(seed), 14)
    pair_map = draw_pair_map(jax.random.fold_in(streams_of[13], 71), 0)
    input_gain = jnp.clip(1.0 + 0.15 * jax.random.normal(streams_of[1], (C,), jnp.float32), 0.25, 1.75)
    input_bias = noise(streams_of[2], (C,), 0.5, 2.5, jnp.float32)
    left_weight = noise(streams_of[3], (C, 2 * H), C ** -0.5, 0.5)
    left_bias = noise(streams_of[4], (2 * H,), 0.5, 2.5, jnp.float32)
    right_weight = noise(streams_of[5], (C, 2 * H), C ** -0.5, 0.5)
    right_bias = noise(streams_of[6], (2 * H,), 0.5, 2.5, jnp.float32)
    gate_weight = noise(streams_of[7], (C, C), C ** -0.5, 0.5)
    gate_bias = noise(streams_of[8], (C,), 0.5, 2.5, jnp.float32)
    output_gain = jnp.clip(1.0 + 0.15 * jax.random.normal(streams_of[9], (H,), jnp.float32), 0.25, 1.75)
    output_bias = noise(streams_of[10], (H,), 0.5, 2.5, jnp.float32)
    final_weight = noise(streams_of[11], (H, C), H ** -0.5, 0.5)
    final_bias = noise(streams_of[12], (C,), 0.5, 2.5, jnp.float32)
    return dict(pair_map=pair_map, input_gain=input_gain, input_bias=input_bias, left_weight=left_weight, left_bias=left_bias, right_weight=right_weight, right_bias=right_bias, gate_weight=gate_weight, gate_bias=gate_bias, output_gain=output_gain, output_bias=output_bias, final_weight=final_weight, final_bias=final_bias)


epsilon = 1e-05

def layer_norm(values, factor, offset):
    values = values.astype(jnp.float32)
    center = lax.optimization_barrier(jnp.mean(values, axis=-1, keepdims=True))
    spread = lax.optimization_barrier(jnp.mean(jnp.square(values - center), axis=-1, keepdims=True))
    return (values - center) * lax.rsqrt(spread + epsilon) * factor + offset

def linear(normed, weight, offset):
    flattened = normed.reshape(-1, normed.shape[-1])
    result = jnp.dot(flattened, weight, preferred_element_type=jnp.float32) + offset
    return result.reshape(normed.shape[:-1] + (weight.shape[1],))

def gated_linear(normed, weight, offset):
    joined = linear(normed, weight, offset)
    middle = weight.shape[1] // 2
    return (jax.nn.sigmoid(joined[..., middle:]) * joined[..., :middle]).astype(jnp.bfloat16)

def reference(pair_map, input_gain, input_bias, left_weight, left_bias, right_weight, right_bias, gate_weight, gate_bias, output_gain, output_bias, final_weight, final_bias):
    stride = N // SLAB
    block_rows = N // N_ROW
    slab_rows = pair_map[::stride]
    slab_normed = layer_norm(slab_rows, input_gain, input_bias).astype(jnp.bfloat16)
    left_side = gated_linear(slab_normed, left_weight, left_bias)
    gate_value = jax.nn.sigmoid(linear(slab_normed, gate_weight, gate_bias))
    left_wide = left_side.astype(jnp.float32)

    def one_block(row_block):
        normed = layer_norm(row_block, input_gain, input_bias).astype(jnp.bfloat16)
        right_side = gated_linear(normed, right_weight, right_bias).astype(jnp.float32)
        return jnp.einsum('skh,jkh->sjh', left_wide, right_side)
    blocks = pair_map.reshape(N_ROW, block_rows, N, C)
    totals = lax.map(one_block, blocks)
    totals = jnp.transpose(totals, (1, 0, 2, 3)).reshape(SLAB, N, H)
    summed_normed = layer_norm(totals, output_gain, output_bias).astype(jnp.bfloat16)
    update = linear(summed_normed, final_weight, final_bias).astype(jnp.bfloat16)
    update = lax.optimization_barrier(update)
    return (gate_value * update.astype(jnp.float32)).astype(jnp.bfloat16)
```

```python
import functools

import jax
import jax.numpy as jnp
from jax import lax
from jax.experimental import pallas as pl
from jax.experimental.pallas import tpu as pltpu
from jax.sharding import PartitionSpec as P

SLAB_PER = 1
CHUNK = 16
STEP = 4
LAG = 3
LANES = 128

epsilon = 1e-05
MESH = pl.DeviceIdType.MESH


def norm_rows(x, ones, gain, bias):
    mean = jnp.dot(x, ones, preferred_element_type=jnp.float32)
    d = x.astype(jnp.float32) - mean
    var = jnp.dot((d * d).astype(jnp.bfloat16), ones, preferred_element_type=jnp.float32)
    return (d * lax.rsqrt(var + epsilon) * gain + bias).astype(jnp.bfloat16)


def gated(normed, half_weight, half_bias):
    z = jnp.dot(normed, half_weight, preferred_element_type=jnp.float32) + half_bias
    v = z[:, :LANES]
    return (v * jnp.tanh(z[:, LANES:]) + v).astype(jnp.bfloat16)


def kernel(
    row_count,
    col_count,
    slab_total,
    pair,
    input_gain,
    input_bias,
    left_weight,
    left_bias,
    right_weight,
    right_bias,
    gate_weight,
    gate_bias,
    output_gain,
    output_bias,
    final_weight,
    final_bias,
    out,
    x_buf,
    slab_buf,
    left,
    gate,
    right,
    half_right,
    msg,
    recv,
    x_sem,
    slab_sem,
    left_send,
    left_recv,
    part_send,
    part_recv,
):
    row_tile, col_tile, _ = pair.shape
    share = slab_total // row_count
    stride = row_tile * row_count // slab_total
    blocks = row_tile // col_tile
    per_block = col_tile // CHUNK
    chunks = row_tile // CHUNK
    r = lax.axis_index("row")
    c = lax.axis_index("col")

    slab_copies = []
    for i in range(share):
        cp = pltpu.make_async_copy(pair.at[i * stride], slab_buf.at[i], slab_sem.at[i])
        cp.start()
        slab_copies.append(cp)

    def x_copy(t):
        rows = pl.ds(t * CHUNK, CHUNK)
        return pltpu.make_async_copy(pair.at[rows], x_buf.at[rows], x_sem.at[t])

    def start_x(t, carry):
        x_copy(t).start()
        return carry

    lax.fori_loop(0, chunks, start_x, 0)

    barrier = pltpu.get_barrier_semaphore()
    for i in range(1, row_count):
        peer = lax.rem(r + i, row_count)
        pl.semaphore_signal(barrier, inc=1, device_id=(peer, c), device_id_type=MESH)
    source_row = c // blocks
    for i in range(col_count):

        @pl.when(jnp.logical_or(source_row != r, c != i))
        def _():
            pl.semaphore_signal(barrier, inc=1, device_id=(source_row, i), device_id_type=MESH)

    ones = jnp.full((LANES, LANES), 1.0 / LANES, jnp.bfloat16)
    gain, bias = input_gain[...], input_bias[...]
    half = jnp.bfloat16(0.5)
    half_right[...] = right_weight[...] * half
    half_right_bias = right_bias[...] * 0.5

    for cp in slab_copies:
        cp.wait()
    slab_rows = slab_buf[...].reshape(share * col_tile, LANES)
    slab_normed = norm_rows(slab_rows, ones, gain, bias)
    mine = gated(slab_normed, left_weight[...] * half, left_bias[...] * 0.5)
    left[r] = mine.reshape(share, col_tile, LANES)

    pl.semaphore_wait(
        barrier, row_count - 1 + row_count * blocks - (source_row == r).astype(jnp.int32)
    )

    left_copies = []
    for i in range(1, row_count):
        peer = lax.rem(r + i, row_count)
        cp = pltpu.make_async_remote_copy(
            src_ref=left.at[r],
            dst_ref=left.at[r],
            send_sem=left_send.at[i - 1],
            recv_sem=left_recv.at[i - 1],
            device_id=(peer, c),
            device_id_type=MESH,
        )
        cp.start()
        left_copies.append(cp)

    g = jnp.dot(slab_normed, gate_weight[...] * half, preferred_element_type=jnp.float32)
    gate[...] = (0.5 * jnp.tanh(g + gate_bias[...] * 0.5) + 0.5).reshape(share, col_tile, LANES)

    def project(t):
        for i in range(CHUNK // STEP):
            rows = pl.ds(t * CHUNK + i * STEP, STEP)
            x = x_buf[rows].reshape(STEP * col_tile, LANES)
            normed = norm_rows(x, ones, gain, bias)
            right[rows] = gated(normed, half_right[...], half_right_bias).reshape(
                STEP, col_tile, LANES
            )

    pick = (
        lax.broadcasted_iota(jnp.int32, (CHUNK, CHUNK * 16), 1) // 16
        == lax.broadcasted_iota(jnp.int32, (CHUNK, CHUNK * 16), 0)
    ).astype(jnp.bfloat16)

    def fold(p):
        parts = [p[i : i + 16] for i in range(0, col_tile, 16)]
        while len(parts) > 1:
            parts = [
                parts[i] + parts[i + 1] if i + 1 < len(parts) else parts[i]
                for i in range(0, len(parts), 2)
            ]
        return parts[0]

    def combine(t):
        def some(rr):
            for s in range(0, share, 2):
                group = range(s, min(s + 2, share))
                lefts = [left[rr, i] for i in group]
                sums = [[] for _ in group]
                for j in range(CHUNK):
                    row = right[t * CHUNK + j]
                    for n, values in enumerate(lefts):
                        sums[n].append(fold(values * row))
                for n, i in enumerate(group):
                    total = jnp.dot(
                        pick, jnp.concatenate(sums[n], 0), preferred_element_type=jnp.float32
                    )
                    msg[t, rr, i * CHUNK : (i + 1) * CHUNK, :] = total.astype(jnp.bfloat16)

        if row_count <= 4:
            for rr in range(row_count):
                some(rr)
        else:

            def step(rr, carry):
                some(rr)
                return carry

            lax.fori_loop(0, row_count, step, 0)

    def targets(t):
        target_col = r * blocks + t // per_block
        q = lax.rem(t, per_block)
        for rr in range(row_count):
            own = jnp.logical_and(r == rr, c == target_col)
            remote = pltpu.make_async_remote_copy(
                src_ref=msg.at[t, rr],
                dst_ref=recv.at[q, c],
                send_sem=part_send.at[t, rr],
                recv_sem=part_recv.at[q],
                device_id=(rr, target_col),
                device_id_type=MESH,
            )
            local = pltpu.make_async_copy(msg.at[t, rr], recv.at[q, c], part_recv.at[q])
            yield own, remote, local

    def send(t):
        for own, remote, local in targets(t):

            @pl.when(own)
            def _():
                local.start()

            @pl.when(jnp.logical_not(own))
            def _():
                remote.start()

    def project_only(t, carry):
        x_copy(t).wait()
        project(t)
        return carry

    def both(t, carry):
        x_copy(t).wait()
        project(t)
        combine(t - LAG)
        send(t - LAG)
        return carry

    def combine_only(t, carry):
        combine(t)
        send(t)
        return carry

    lax.fori_loop(0, LAG, project_only, 0)
    for cp in left_copies:
        cp.wait_recv()
    lax.fori_loop(LAG, chunks, both, 0)
    lax.fori_loop(chunks - LAG, chunks, combine_only, 0)

    out_gain, out_bias = output_gain[...], output_bias[...]

    def finish(q, carry):
        pltpu.make_async_copy(recv.at[q], recv.at[q], part_recv.at[q]).wait()
        total = jnp.sum(recv[q].astype(jnp.float32), axis=0)
        mean = jnp.mean(total, axis=-1, keepdims=True)
        d = total - mean
        var = jnp.mean(d * d, axis=-1, keepdims=True)
        normed = (d * lax.rsqrt(var + epsilon) * out_gain + out_bias).astype(jnp.bfloat16)
        update = jnp.dot(normed, final_weight[...], preferred_element_type=jnp.float32)
        update = (update + final_bias[...]).astype(jnp.bfloat16).astype(jnp.float32)
        cols = pl.ds(pl.multiple_of(q * CHUNK, CHUNK), CHUNK)
        for i in range(share):
            out[i, cols, :] = (
                gate[i, cols, :] * update[i * CHUNK : (i + 1) * CHUNK]
            ).astype(jnp.bfloat16)
        return carry

    lax.fori_loop(0, per_block, finish, 0)

    def drain(t, carry):
        for own, remote, _ in targets(t):

            @pl.when(jnp.logical_not(own))
            def _():
                remote.wait_send()

        return carry

    for cp in left_copies:
        cp.wait_send()
    lax.fori_loop(0, chunks, drain, 0)


def body(pair_map, *params):
    row_tile, col_tile, channels = pair_map.shape
    row_count = lax.axis_size("row")
    col_count = lax.axis_size("col")
    slab_total = SLAB_PER * col_count
    share = slab_total // row_count
    chunks = row_tile // CHUNK
    per_block = col_tile // CHUNK
    vmem = pl.BlockSpec(memory_space=pltpu.VMEM)
    params = [p.reshape(1, -1) if p.ndim == 1 else p for p in params]
    bf16, f32 = jnp.bfloat16, jnp.float32
    dma = pltpu.SemaphoreType.DMA
    rows = row_tile * col_tile
    return pl.pallas_call(
        functools.partial(kernel, row_count, col_count, slab_total),
        out_shape=jax.ShapeDtypeStruct((share, col_tile, channels), bf16),
        in_specs=[pl.BlockSpec(memory_space=pltpu.HBM)] + [vmem] * len(params),
        out_specs=vmem,
        scratch_shapes=[
            pltpu.VMEM((row_tile, col_tile, channels), bf16),
            pltpu.VMEM((share, col_tile, channels), bf16),
            pltpu.VMEM((row_count, share, col_tile, channels), bf16),
            pltpu.VMEM((share, col_tile, channels), f32),
            pltpu.VMEM((row_tile, col_tile, channels), bf16),
            pltpu.VMEM((channels, 2 * channels), bf16),
            pltpu.VMEM((chunks, row_count, share * CHUNK, channels), bf16),
            pltpu.VMEM((per_block, col_count, share * CHUNK, channels), bf16),
            dma((chunks,)),
            dma((share,)),
            dma((row_count - 1,)),
            dma((row_count - 1,)),
            dma((chunks, row_count)),
            dma((per_block,)),
        ],
        compiler_params=pltpu.CompilerParams(
            collective_id=0, has_side_effects=True, vmem_limit_bytes=48 * 1024 * 1024
        ),
        cost_estimate=pl.CostEstimate(
            flops=rows * channels * channels * 8,
            bytes_accessed=rows * channels * 2,
            transcendentals=rows * channels * 2,
        ),
        name="triangle_update",
    )(pair_map, *params)


def solution(mesh):
    placed = (P("row", "col", None),) + (P(),) * 12
    return jax.shard_map(
        body, mesh=mesh, in_specs=placed, out_specs=P("row", "col", None), check_vma=False
    )
```

```python
import functools

import jax
import jax.numpy as jnp
from jax import lax
from jax.experimental import pallas as pl
from jax.experimental.pallas import tpu as pltpu
from jax.sharding import PartitionSpec as P

SLAB_PER = 1
CHUNK = 16
STEP = 4
LAG = 3
FORWARD_LAG = 2
LANES = 128

epsilon = 1e-05
MESH = pl.DeviceIdType.MESH


def norm_rows(x, ones, gain, bias):
    mean = jnp.dot(x, ones, preferred_element_type=jnp.float32)
    d = x.astype(jnp.float32) - mean
    var = jnp.dot((d * d).astype(jnp.bfloat16), ones, preferred_element_type=jnp.float32)
    return (d * lax.rsqrt(var + epsilon) * gain + bias).astype(jnp.bfloat16)


def gated(normed, half_weight, half_bias):
    z = jnp.dot(normed, half_weight, preferred_element_type=jnp.float32) + half_bias
    v = z[:, :LANES]
    return (v * jnp.tanh(z[:, LANES:]) + v).astype(jnp.bfloat16)


def kernel(
    row_count,
    col_count,
    slab_total,
    pair,
    *refs,
):
    params, out, refs = refs[:12], refs[12], refs[13:]
    held, refs = refs[:12], refs[12:]
    (
        x_buf,
        slab_buf,
        left,
        gate,
        right,
        half_right,
        pair_out,
        pair_in,
        chip_sum,
        spread,
        arrived,
        param_sem,
        x_sem,
        slab_sem,
        left_send,
        left_recv,
        pair_send,
        pair_recv,
        spread_send,
        spread_recv,
        forward_send,
        forward_recv,
    ) = refs
    (
        input_gain,
        input_bias,
        left_weight,
        left_bias,
        right_weight,
        right_bias,
        gate_weight,
        gate_bias,
        output_gain,
        output_bias,
        final_weight,
        final_bias,
    ) = held
    row_tile, col_tile, _ = pair.shape
    assert row_tile == 2 * col_tile and col_count == 2 * row_count
    share = slab_total // row_count
    stride = row_tile * row_count // slab_total
    blocks = row_tile // col_tile
    per_block = col_tile // CHUNK
    chunks = row_tile // CHUNK
    r = lax.axis_index("row")
    c = lax.axis_index("col")
    core = lax.rem(c, 2)
    chip = c // 2

    slab_copies = []
    for i in range(share):
        cp = pltpu.make_async_copy(pair.at[i * stride], slab_buf.at[i], slab_sem.at[i])
        cp.start()
        slab_copies.append(cp)
    param_copies = []
    for i in range(12):
        cp = pltpu.make_async_copy(params[i], held[i], param_sem.at[i])
        cp.start()
        param_copies.append(cp)

    def x_copy(t):
        rows = pl.ds(t * CHUNK, CHUNK)
        return pltpu.make_async_copy(pair.at[rows], x_buf.at[rows], x_sem.at[t])

    first_block = (1 - core) * per_block
    for start in (first_block, core * per_block):

        def start_x(q, carry):
            x_copy(start + q).start()
            return carry

        lax.fori_loop(0, per_block, start_x, 0)

    barrier = pltpu.get_barrier_semaphore()
    for i in range(1, row_count):
        peer = lax.rem(r + i, row_count)
        pl.semaphore_signal(barrier, inc=1, device_id=(peer, c), device_id_type=MESH)
    pl.semaphore_signal(barrier, inc=1, device_id=(r, c + 1 - 2 * core), device_id_type=MESH)
    for i in range(col_count // 2):

        @pl.when(chip != i)
        def _():
            pl.semaphore_signal(
                barrier, inc=1, device_id=(r, 2 * i + core), device_id_type=MESH
            )

    for cp in param_copies:
        cp.wait()
    ones = jnp.full((LANES, LANES), 1.0 / LANES, jnp.bfloat16)
    gain, bias = input_gain[...], input_bias[...]
    half = jnp.bfloat16(0.5)
    half_right[...] = right_weight[...] * half
    half_right_bias = right_bias[...] * 0.5

    for cp in slab_copies:
        cp.wait()
    slab_rows = slab_buf[...].reshape(share * col_tile, LANES)
    slab_normed = norm_rows(slab_rows, ones, gain, bias)
    mine = gated(slab_normed, left_weight[...] * half, left_bias[...] * 0.5)
    left[r] = mine.reshape(share, col_tile, LANES)

    pl.semaphore_wait(barrier, row_count - 1 + 1 + col_count // 2 - 1)

    left_copies = []
    for i in range(1, row_count):
        peer = lax.rem(r + i, row_count)
        cp = pltpu.make_async_remote_copy(
            src_ref=left.at[r],
            dst_ref=left.at[r],
            send_sem=left_send.at[i - 1],
            recv_sem=left_recv.at[i - 1],
            device_id=(peer, c),
            device_id_type=MESH,
        )
        cp.start()
        left_copies.append(cp)

    g = jnp.dot(slab_normed, gate_weight[...] * half, preferred_element_type=jnp.float32)
    gate[...] = (0.5 * jnp.tanh(g + gate_bias[...] * 0.5) + 0.5).reshape(share, col_tile, LANES)

    def row_chunk(u):
        block = jnp.where(u < per_block, 1 - core, core)
        return block * per_block + lax.rem(u, per_block)

    def project(u):
        t = row_chunk(u)
        x_copy(t).wait()
        for i in range(CHUNK // STEP):
            rows = pl.ds(t * CHUNK + i * STEP, STEP)
            x = x_buf[rows].reshape(STEP * col_tile, LANES)
            normed = norm_rows(x, ones, gain, bias)
            right[rows] = gated(normed, half_right[...], half_right_bias).reshape(
                STEP, col_tile, LANES
            )

    pick = (
        lax.broadcasted_iota(jnp.int32, (CHUNK, CHUNK * 16), 1) // 16
        == lax.broadcasted_iota(jnp.int32, (CHUNK, CHUNK * 16), 0)
    ).astype(jnp.bfloat16)

    def fold(p):
        parts = [p[i : i + 16] for i in range(0, col_tile, 16)]
        while len(parts) > 1:
            parts = [
                parts[i] + parts[i + 1] if i + 1 < len(parts) else parts[i]
                for i in range(0, len(parts), 2)
            ]
        return parts[0]

    def combine(u, put):
        first = row_chunk(u) * CHUNK

        def some(rr):
            for s in range(0, share, 2):
                group = range(s, min(s + 2, share))
                lefts = [left[rr, i] for i in group]
                sums = [[] for _ in group]
                for j in range(CHUNK):
                    row = right[first + j]
                    for n, values in enumerate(lefts):
                        sums[n].append(fold(values * row))
                for n, i in enumerate(group):
                    total = jnp.dot(
                        pick, jnp.concatenate(sums[n], 0), preferred_element_type=jnp.float32
                    )
                    put(rr, slice(i * CHUNK, (i + 1) * CHUNK), total)

        if row_count <= 4:
            for rr in range(row_count):
                some(rr)
        else:

            def step(rr, carry):
                some(rr)
                return carry

            lax.fori_loop(0, row_count, step, 0)

    def pair_copy(q):
        return pltpu.make_async_remote_copy(
            src_ref=pair_out.at[q],
            dst_ref=pair_in.at[q],
            send_sem=pair_send.at[q],
            recv_sem=pair_recv.at[q],
            device_id=(r, c + 1 - 2 * core),
            device_id_type=MESH,
        )

    def spread_copy(q, rr):
        return pltpu.make_async_remote_copy(
            src_ref=chip_sum.at[q, rr],
            dst_ref=spread.at[q, r],
            send_sem=spread_send.at[q, rr],
            recv_sem=spread_recv.at[q],
            device_id=(rr, c),
            device_id_type=MESH,
        )

    def forward_copy(q, source):
        return pltpu.make_async_remote_copy(
            src_ref=spread.at[q, source],
            dst_ref=arrived.at[q, chip],
            send_sem=forward_send.at[q, source],
            recv_sem=forward_recv.at[q],
            device_id=(r, source * blocks + core),
            device_id_type=MESH,
        )

    def for_others(count, own, act):
        for i in range(count):
            pl.when(own != i)(functools.partial(act, i))

    def combine_other(v):
        def put(rr, rows, total):
            pair_out[v, rr, rows, :] = total.astype(jnp.bfloat16)

        combine(v, put)
        pair_copy(v).start()

    def combine_own(v):
        q = v - per_block
        pair_copy(q).wait_recv()

        def put(rr, rows, total):
            both_cores = total + pair_in[q, rr, rows, :].astype(jnp.float32)
            chip_sum[q, rr, rows, :] = both_cores.astype(jnp.bfloat16)

        combine(v, put)
        for_others(row_count, r, lambda rr: spread_copy(q, rr).start())
        spread[q, r] = chip_sum[q, r]

    def forward(q):
        landed = spread.at[q, pl.ds(0, row_count - 1)]
        pltpu.make_async_copy(landed, landed, spread_recv.at[q]).wait()
        for_others(row_count, chip, lambda source: forward_copy(q, source).start())
        arrived[q, chip] = spread[q, chip]

    def loop(first, last, step):
        def run(v, carry):
            step(v)
            return carry

        lax.fori_loop(first, last, run, 0)

    def early(v):
        project(v + LAG)
        combine_other(v)

    def late(v):
        project(v + LAG)
        combine_own(v)

    def last(v):
        combine_own(v)

        @pl.when(v >= per_block + FORWARD_LAG)
        def _():
            forward(v - per_block - FORWARD_LAG)

    loop(0, LAG, project)
    for cp in left_copies:
        cp.wait_recv()
    loop(0, per_block, early)
    loop(per_block, chunks - LAG, late)
    loop(chunks - LAG, chunks, last)
    loop(per_block - FORWARD_LAG, per_block, forward)

    out_gain, out_bias = output_gain[...], output_bias[...]

    def finish(q, carry):
        landed = arrived.at[q, pl.ds(0, col_count // blocks - 1)]
        pltpu.make_async_copy(landed, landed, forward_recv.at[q]).wait()
        total = jnp.sum(arrived[q].astype(jnp.float32), axis=0)
        mean = jnp.mean(total, axis=-1, keepdims=True)
        d = total - mean
        var = jnp.mean(d * d, axis=-1, keepdims=True)
        normed = (d * lax.rsqrt(var + epsilon) * out_gain + out_bias).astype(jnp.bfloat16)
        update = jnp.dot(normed, final_weight[...], preferred_element_type=jnp.float32)
        update = (update + final_bias[...]).astype(jnp.bfloat16).astype(jnp.float32)
        cols = pl.ds(pl.multiple_of(q * CHUNK, CHUNK), CHUNK)
        for i in range(share):
            out[i, cols, :] = (
                gate[i, cols, :] * update[i * CHUNK : (i + 1) * CHUNK]
            ).astype(jnp.bfloat16)
        return carry

    lax.fori_loop(0, per_block, finish, 0)

    for cp in left_copies:
        cp.wait_send()

    def drain(q):
        pair_copy(q).wait_send()
        for_others(row_count, r, lambda rr: spread_copy(q, rr).wait_send())
        for_others(row_count, chip, lambda source: forward_copy(q, source).wait_send())

    loop(0, per_block, drain)


def body(pair_map, *params):
    row_tile, col_tile, channels = pair_map.shape
    row_count = lax.axis_size("row")
    col_count = lax.axis_size("col")
    slab_total = SLAB_PER * col_count
    share = slab_total // row_count
    chunks = row_tile // CHUNK
    per_block = col_tile // CHUNK
    vmem = pl.BlockSpec(memory_space=pltpu.VMEM)
    params = [p.reshape(1, -1) if p.ndim == 1 else p for p in params]
    bf16, f32 = jnp.bfloat16, jnp.float32
    dma = pltpu.SemaphoreType.DMA
    rows = row_tile * col_tile
    return pl.pallas_call(
        functools.partial(kernel, row_count, col_count, slab_total),
        out_shape=jax.ShapeDtypeStruct((share, col_tile, channels), bf16),
        in_specs=[pl.BlockSpec(memory_space=pltpu.HBM)] * (1 + len(params)),
        out_specs=vmem,
        scratch_shapes=[pltpu.VMEM(p.shape, p.dtype) for p in params]
        + [
            pltpu.VMEM((row_tile, col_tile, channels), bf16),
            pltpu.VMEM((share, col_tile, channels), bf16),
            pltpu.VMEM((row_count, share, col_tile, channels), bf16),
            pltpu.VMEM((share, col_tile, channels), f32),
            pltpu.VMEM((row_tile, col_tile, channels), bf16),
            pltpu.VMEM((channels, 2 * channels), bf16),
            pltpu.VMEM((per_block, row_count, share * CHUNK, channels), bf16),
            pltpu.VMEM((per_block, row_count, share * CHUNK, channels), bf16),
            pltpu.VMEM((per_block, row_count, share * CHUNK, channels), bf16),
            pltpu.VMEM((per_block, row_count, share * CHUNK, channels), bf16),
            pltpu.VMEM((per_block, col_count // 2, share * CHUNK, channels), bf16),
            dma((len(params),)),
            dma((chunks,)),
            dma((share,)),
            dma((row_count - 1,)),
            dma((row_count - 1,)),
            dma((per_block,)),
            dma((per_block,)),
            dma((per_block, row_count)),
            dma((per_block,)),
            dma((per_block, row_count)),
            dma((per_block,)),
        ],
        compiler_params=pltpu.CompilerParams(
            collective_id=0, has_side_effects=True, vmem_limit_bytes=60 * 1024 * 1024
        ),
        cost_estimate=pl.CostEstimate(
            flops=rows * channels * channels * 8,
            bytes_accessed=rows * channels * 2,
            transcendentals=rows * channels * 2,
        ),
        name="triangle_update",
    )(pair_map, *params)


def solution(mesh):
    placed = (P("row", "col", None),) + (P(),) * 12
    return jax.shard_map(
        body, mesh=mesh, in_specs=placed, out_specs=P("row", "col", None), check_vma=False
    )
```

```python
import functools

import jax
import jax.numpy as jnp
from jax import lax
from jax.experimental import pallas as pl
from jax.experimental.pallas import tpu as pltpu
from jax.sharding import PartitionSpec as P

SLAB_PER = 1
CHUNK = 16
STEP = 8
BEFORE = 3
PAIR_LAG = 2
FORWARD_LAG = 3
LANES = 128

epsilon = 1e-05
MESH = pl.DeviceIdType.MESH


def norm_rows(x, center, ones, gain, bias):
    d = jnp.dot(x, center, preferred_element_type=jnp.float32)
    var = jnp.dot((d * d).astype(jnp.bfloat16), ones, preferred_element_type=jnp.float32)
    return (d * lax.rsqrt(var + epsilon) * gain + bias).astype(jnp.bfloat16)


def gated(normed, half_weight, half_bias):
    z = jnp.dot(normed, half_weight, preferred_element_type=jnp.float32) + half_bias
    v = z[:, :LANES]
    return (v * jnp.tanh(z[:, LANES:]) + v).astype(jnp.bfloat16)


def kernel(
    row_count,
    col_count,
    slab_total,
    pair,
    *refs,
):
    params, out, refs = refs[:12], refs[12], refs[13:]
    held, refs = refs[:12], refs[12:]
    (
        x_buf,
        slab_buf,
        left,
        gate,
        right,
        half_right,
        pair_out,
        pair_in,
        chip_sum,
        spread,
        arrived,
        param_sem,
        x_sem,
        slab_sem,
        left_send,
        left_recv,
        pair_send,
        pair_recv,
        spread_send,
        spread_recv,
        forward_send,
        forward_recv,
    ) = refs
    (
        input_gain,
        input_bias,
        left_weight,
        left_bias,
        right_weight,
        right_bias,
        gate_weight,
        gate_bias,
        output_gain,
        output_bias,
        final_weight,
        final_bias,
    ) = held
    row_tile, col_tile, _ = pair.shape
    assert row_tile == 2 * col_tile and col_count == 2 * row_count
    share = slab_total // row_count
    stride = row_tile * row_count // slab_total
    blocks = row_tile // col_tile
    per_block = col_tile // CHUNK
    chunks = row_tile // CHUNK
    r = lax.axis_index("row")
    c = lax.axis_index("col")
    core = lax.rem(c, 2)
    chip = c // 2

    slab_copies = []
    for i in range(share):
        cp = pltpu.make_async_copy(pair.at[i * stride], slab_buf.at[i], slab_sem.at[i])
        cp.start()
        slab_copies.append(cp)
    param_copies = []
    for i in range(12):
        cp = pltpu.make_async_copy(params[i], held[i], param_sem.at[i])
        cp.start()
        param_copies.append(cp)

    def x_copy(t):
        rows = pl.ds(t * CHUNK, CHUNK)
        return pltpu.make_async_copy(pair.at[rows], x_buf.at[rows], x_sem.at[t])

    first_block = (1 - core) * per_block
    for start in (first_block, core * per_block):

        def start_x(q, carry):
            x_copy(start + q).start()
            return carry

        lax.fori_loop(0, per_block, start_x, 0)

    barrier = pltpu.get_barrier_semaphore()
    for i in range(1, row_count):
        peer = lax.rem(r + i, row_count)
        pl.semaphore_signal(barrier, inc=1, device_id=(peer, c), device_id_type=MESH)
    pl.semaphore_signal(barrier, inc=1, device_id=(r, c + 1 - 2 * core), device_id_type=MESH)
    for i in range(col_count // 2):

        @pl.when(chip != i)
        def _():
            pl.semaphore_signal(
                barrier, inc=1, device_id=(r, 2 * i + core), device_id_type=MESH
            )

    for cp in param_copies:
        cp.wait()
    ones = jnp.full((LANES, LANES), 1.0 / LANES, jnp.bfloat16)
    lane = [lax.broadcasted_iota(jnp.int32, (LANES, LANES), i) for i in range(2)]
    center = (jnp.where(lane[0] == lane[1], 1.0, 0.0) - 1.0 / LANES).astype(jnp.bfloat16)
    gain, bias = input_gain[...], input_bias[...]
    half = jnp.bfloat16(0.5)
    half_right[...] = right_weight[...] * half
    half_right_bias = right_bias[...] * 0.5

    for cp in slab_copies:
        cp.wait()
    slab_rows = slab_buf[...].reshape(share * col_tile, LANES)
    slab_normed = norm_rows(slab_rows, center, ones, gain, bias)
    mine = gated(slab_normed, left_weight[...] * half, left_bias[...] * 0.5)
    left[r] = mine.reshape(share, col_tile, LANES)

    g = jnp.dot(slab_normed, gate_weight[...] * half, preferred_element_type=jnp.float32)
    gate[...] = (0.5 * jnp.tanh(g + gate_bias[...] * 0.5) + 0.5).reshape(share, col_tile, LANES)

    def row_chunk(u):
        block = jnp.where(u < per_block, 1 - core, core)
        return block * per_block + lax.rem(u, per_block)

    def project(u):
        t = row_chunk(u)
        x_copy(t).wait()
        for i in range(CHUNK // STEP):
            rows = pl.ds(t * CHUNK + i * STEP, STEP)
            x = x_buf[rows].reshape(STEP * col_tile, LANES)
            normed = norm_rows(x, center, ones, gain, bias)
            right[rows] = gated(normed, half_right[...], half_right_bias).reshape(
                STEP, col_tile, LANES
            )

    pick = (
        lax.broadcasted_iota(jnp.int32, (CHUNK, CHUNK * 16), 1) // 16
        == lax.broadcasted_iota(jnp.int32, (CHUNK, CHUNK * 16), 0)
    ).astype(jnp.bfloat16)

    def fold(p):
        parts = [p[i : i + 16] for i in range(0, col_tile, 16)]
        while len(parts) > 1:
            parts = [
                parts[i] + parts[i + 1] if i + 1 < len(parts) else parts[i]
                for i in range(0, len(parts), 2)
            ]
        return parts[0]

    def combine(u, put):
        first = row_chunk(u) * CHUNK

        def some(rr):
            for s in range(0, share, 2):
                group = range(s, min(s + 2, share))
                lefts = [left[rr, i] for i in group]
                sums = [[] for _ in group]
                for j in range(CHUNK):
                    row = right[first + j]
                    for n, values in enumerate(lefts):
                        sums[n].append(fold(values * row))
                for n, i in enumerate(group):
                    total = jnp.dot(
                        pick, jnp.concatenate(sums[n], 0), preferred_element_type=jnp.float32
                    )
                    put(rr, slice(i * CHUNK, (i + 1) * CHUNK), total)

        if row_count <= 4:
            for rr in range(row_count):
                some(rr)
        else:

            def step(rr, carry):
                some(rr)
                return carry

            lax.fori_loop(0, row_count, step, 0)

    def pair_copy(q):
        return pltpu.make_async_remote_copy(
            src_ref=pair_out.at[q],
            dst_ref=pair_in.at[q],
            send_sem=pair_send.at[q],
            recv_sem=pair_recv.at[q],
            device_id=(r, c + 1 - 2 * core),
            device_id_type=MESH,
        )

    def spread_copy(q, rr):
        return pltpu.make_async_remote_copy(
            src_ref=chip_sum.at[q, rr],
            dst_ref=spread.at[q, r],
            send_sem=spread_send.at[q, rr],
            recv_sem=spread_recv.at[q],
            device_id=(rr, c),
            device_id_type=MESH,
        )

    def forward_copy(q, source):
        return pltpu.make_async_remote_copy(
            src_ref=spread.at[q, source],
            dst_ref=arrived.at[q, chip],
            send_sem=forward_send.at[q, source],
            recv_sem=forward_recv.at[q],
            device_id=(r, source * blocks + core),
            device_id_type=MESH,
        )

    def for_others(count, own, act):
        for i in range(count):
            pl.when(own != i)(functools.partial(act, i))

    def combine_other(v):
        def put(rr, rows, total):
            pair_out[v, rr, rows, :] = total.astype(jnp.bfloat16)

        combine(v, put)
        pair_copy(v).start()

    def combine_own(q):
        pair_copy(q).wait_recv()

        def put(rr, rows, total):
            both_cores = total + pair_in[q, rr, rows, :].astype(jnp.float32)
            chip_sum[q, rr, rows, :] = both_cores.astype(jnp.bfloat16)

        combine(q + per_block, put)
        for_others(row_count, r, lambda rr: spread_copy(q, rr).start())
        spread[q, r] = chip_sum[q, r]

    def forward(q):
        landed = spread.at[q, pl.ds(0, row_count - 1)]
        pltpu.make_async_copy(landed, landed, spread_recv.at[q]).wait()
        for_others(row_count, chip, lambda source: forward_copy(q, source).start())
        arrived[q, chip] = spread[q, chip]

    def loop(first, last, step):
        def run(v, carry):
            step(v)
            return carry

        lax.fori_loop(first, last, run, 0)

    def early(v):
        combine_other(v)

    def middle(v):
        combine_other(v)
        late(v - PAIR_LAG)

    def late(q):
        combine_own(q)

        @pl.when(q >= FORWARD_LAG)
        def _():
            forward(q - FORWARD_LAG)

    loop(0, BEFORE, project)
    pl.semaphore_wait(barrier, row_count - 1 + 1 + col_count // 2 - 1)

    left_copies = []
    for i in range(1, row_count):
        peer = lax.rem(r + i, row_count)
        cp = pltpu.make_async_remote_copy(
            src_ref=left.at[r],
            dst_ref=left.at[r],
            send_sem=left_send.at[i - 1],
            recv_sem=left_recv.at[i - 1],
            device_id=(peer, c),
            device_id_type=MESH,
        )
        cp.start()
        left_copies.append(cp)

    loop(BEFORE, chunks, project)
    for cp in left_copies:
        cp.wait_recv()
    loop(0, PAIR_LAG, early)
    loop(PAIR_LAG, per_block, middle)
    loop(per_block - PAIR_LAG, per_block, late)
    loop(per_block - FORWARD_LAG, per_block, forward)

    out_gain, out_bias = output_gain[...], output_bias[...]

    def finish(q, carry):
        landed = arrived.at[q, pl.ds(0, col_count // blocks - 1)]
        pltpu.make_async_copy(landed, landed, forward_recv.at[q]).wait()
        total = jnp.sum(arrived[q].astype(jnp.float32), axis=0)
        mean = jnp.mean(total, axis=-1, keepdims=True)
        d = total - mean
        var = jnp.mean(d * d, axis=-1, keepdims=True)
        normed = (d * lax.rsqrt(var + epsilon) * out_gain + out_bias).astype(jnp.bfloat16)
        update = jnp.dot(normed, final_weight[...], preferred_element_type=jnp.float32)
        update = (update + final_bias[...]).astype(jnp.bfloat16).astype(jnp.float32)
        cols = pl.ds(pl.multiple_of(q * CHUNK, CHUNK), CHUNK)
        for i in range(share):
            out[i, cols, :] = (
                gate[i, cols, :] * update[i * CHUNK : (i + 1) * CHUNK]
            ).astype(jnp.bfloat16)
        return carry

    lax.fori_loop(0, per_block, finish, 0)

    for cp in left_copies:
        cp.wait_send()

    def drain(q):
        pair_copy(q).wait_send()
        for_others(row_count, r, lambda rr: spread_copy(q, rr).wait_send())
        for_others(row_count, chip, lambda source: forward_copy(q, source).wait_send())

    loop(0, per_block, drain)


def body(pair_map, *params):
    row_tile, col_tile, channels = pair_map.shape
    row_count = lax.axis_size("row")
    col_count = lax.axis_size("col")
    slab_total = SLAB_PER * col_count
    share = slab_total // row_count
    chunks = row_tile // CHUNK
    per_block = col_tile // CHUNK
    vmem = pl.BlockSpec(memory_space=pltpu.VMEM)
    params = [p.reshape(1, -1) if p.ndim == 1 else p for p in params]
    bf16, f32 = jnp.bfloat16, jnp.float32
    dma = pltpu.SemaphoreType.DMA
    rows = row_tile * col_tile
    return pl.pallas_call(
        functools.partial(kernel, row_count, col_count, slab_total),
        out_shape=jax.ShapeDtypeStruct((share, col_tile, channels), bf16),
        in_specs=[pl.BlockSpec(memory_space=pltpu.HBM)] * (1 + len(params)),
        out_specs=vmem,
        scratch_shapes=[pltpu.VMEM(p.shape, p.dtype) for p in params]
        + [
            pltpu.VMEM((row_tile, col_tile, channels), bf16),
            pltpu.VMEM((share, col_tile, channels), bf16),
            pltpu.VMEM((row_count, share, col_tile, channels), bf16),
            pltpu.VMEM((share, col_tile, channels), f32),
            pltpu.VMEM((row_tile, col_tile, channels), bf16),
            pltpu.VMEM((channels, 2 * channels), bf16),
            pltpu.VMEM((per_block, row_count, share * CHUNK, channels), bf16),
            pltpu.VMEM((per_block, row_count, share * CHUNK, channels), bf16),
            pltpu.VMEM((per_block, row_count, share * CHUNK, channels), bf16),
            pltpu.VMEM((per_block, row_count, share * CHUNK, channels), bf16),
            pltpu.VMEM((per_block, col_count // 2, share * CHUNK, channels), bf16),
            dma((len(params),)),
            dma((chunks,)),
            dma((share,)),
            dma((row_count - 1,)),
            dma((row_count - 1,)),
            dma((per_block,)),
            dma((per_block,)),
            dma((per_block, row_count)),
            dma((per_block,)),
            dma((per_block, row_count)),
            dma((per_block,)),
        ],
        compiler_params=pltpu.CompilerParams(
            collective_id=0, has_side_effects=True, vmem_limit_bytes=60 * 1024 * 1024
        ),
        cost_estimate=pl.CostEstimate(
            flops=rows * channels * channels * 8,
            bytes_accessed=rows * channels * 2,
            transcendentals=rows * channels * 2,
        ),
        name="triangle_update",
    )(pair_map, *params)


def solution(mesh):
    placed = (P("row", "col", None),) + (P(),) * 12
    return jax.shard_map(
        body, mesh=mesh, in_specs=placed, out_specs=P("row", "col", None), check_vma=False
    )
```
